32 devices in a mesh: slab: 8 (over z, y), blk: 4 (over x, core).
Axes of the slice: x: 2, y: 2, z: 4, core: 2. Of those that a mesh axis runs over, the one named last changes fastest.
Arguments:
- positions: float32 [1024, 3, 128], P(('slab', 'blk')), may hold values from 0 to 1
- radius: float32 [1024, 128], P(('slab', 'blk')), may hold values from 0.15 to 0.3
- velocity: float32 [1024, 3, 128], P(('slab', 'blk')), may hold values from -3 to 3
- old_force: float32 [1024, 3, 128], P(('slab', 'blk')), may hold values from -6 to 6
- neighbours: int32 [1024, 16], P(('slab', 'blk')), may hold values from 0 to 47, as said below
- tile_count: int32 [1024], P(('slab', 'blk')), may hold values from 0 to 16
Outputs:
- new_positions: float32 [1024, 3, 128], P(('slab', 'blk'))
- new_velocity: float32 [1024, 3, 128], P(('slab', 'blk'))
- new_force: float32 [1024, 3, 128], P(('slab', 'blk'))
The draws below stay inside these ranges and needn't reach their ends.
Inputs may be any that keep to these rules, and one draw needn't show every extreme that they name: neighbours[i, k] indexes the candidate list of bin i's group; it never names bin i itself, and names no candidate of a missing slab at the drum's ends.
All inputs are finite; a program needn't handle non-finite values.
Results may differ from the reference program's by a relative error of at most 0.0003.
Values sent between devices are 32-bit elements; how exact they have to be, the bound alone decides.
A program may use at most 64 MiB of HBM per device.

```python
import math
import jax
import jax.numpy as jnp
from jax import lax

SPHERES = 128
SLOTS = 16
GHOSTS = 8
BLOCK_TILES = 32
BINS_DEV = 32
NBINS = 1024
N_SLAB = 8
N_BLK = 4


def draw_tile_count(key, part):
    total_bins = N_SLAB * N_BLK * BINS_DEV
    row_index = jnp.arange(total_bins, dtype=jnp.int32)
    group_index = row_index // BINS_DEV
    slab_index = group_index // N_BLK
    sector = group_index % N_BLK
    offsets = jax.random.randint(jax.random.fold_in(key, 7), (N_SLAB,), 0, N_BLK)
    dense = (sector - offsets[slab_index]) % N_BLK < max(N_BLK // 4, 1)
    ceiling = jnp.where(dense, SLOTS, SLOTS // 4).astype(jnp.int32)
    counts = jax.random.randint(jax.random.fold_in(key, 11), (total_bins,), 0, ceiling + 1)
    first_bin = row_index % BINS_DEV == 0
    counts = jnp.where(first_bin, jnp.where(dense, SLOTS, 0), counts)
    return counts.astype(jnp.int32)


def draw_neighbours(key, part):
    total_bins = N_SLAB * N_BLK * BINS_DEV
    row_index = jnp.arange(total_bins, dtype=jnp.int32)
    slab_index = row_index // BINS_DEV // N_BLK
    local_bin = row_index % BINS_DEV
    lowest = jnp.where(slab_index == 0, GHOSTS, 0).astype(jnp.int32)
    highest = jnp.where(slab_index == N_SLAB - 1, GHOSTS + BINS_DEV, BINS_DEV + 2 * GHOSTS).astype(jnp.int32)
    drawn = jax.random.randint(jax.random.fold_in(key, 13), (total_bins, SLOTS), 0, (highest - lowest - 1)[:, None])
    chosen = lowest[:, None] + drawn
    itself = (GHOSTS + local_bin)[:, None]
    chosen = jnp.where(chosen >= itself, chosen + 1, chosen)
    return chosen.astype(jnp.int32)


def block_scale(stream_key, dims, pieces, smallest, largest):
    def one(position, shards_of):
        steps = jax.random.uniform(jax.random.fold_in(jax.random.fold_in(stream_key, 6), position), (shards_of,), jnp.float32, smallest / len(pieces), largest / len(pieces))
        return jnp.repeat(jnp.exp(steps), dims[position] // shards_of).reshape((-1,) + (1,) * (len(dims) - position - 1))

    level = one(*pieces[0])
    for cut in pieces[1:]:
        level = level * one(*cut)
    return level


def normal_values(own_key, extent, scale, bound, pieces=(), held_as=jnp.bfloat16):
    level = block_scale(own_key, extent, pieces, -0.22, 0.18) if pieces else 1.0
    entries = jax.random.normal(own_key, extent, jnp.float32) * scale * level
    return jnp.minimum(jnp.maximum(entries, -bound), bound).astype(held_as)


def setup_inputs(seed: int = 0) -> dict:
    seeds = jax.random.split(jax.random.key(seed), 7)
    positions = jnp.clip(1.0 * jax.random.uniform(seeds[0], (NBINS, 3, SPHERES), jnp.float32) ** block_scale(seeds[0], (NBINS, 3, SPHERES), ((0, 32),), -0.2, 0.2), 0.0, 1.0)
    radius = jnp.clip(jnp.exp(math.log(0.3) - 0.6931472 * jax.random.uniform(seeds[1], (NBINS, SPHERES), jnp.float32) ** block_scale(seeds[1], (NBINS, SPHERES), ((0, 32),), -0.2, 0.2)), 0.15, 0.3)
    velocity = normal_values(seeds[2], (NBINS, 3, SPHERES), 0.5, 3.0, ((0, 32),), jnp.float32)
    old_force = normal_values(seeds[3], (NBINS, 3, SPHERES), 1.0, 6.0, ((0, 32),), jnp.float32)
    neighbours = draw_neighbours(jax.random.fold_in(seeds[6], 71), 0)
    tile_count = draw_tile_count(jax.random.fold_in(seeds[6], 71), 0)
    return {"positions": positions, "radius": radius, "velocity": velocity, "old_force": old_force, "neighbours": neighbours, "tile_count": tile_count}


STIFFNESS = 10.0
SOFTENING = 0.0025
TIMESTEP = 0.2

def pair_forces(left_tiles, right_tiles):
    offset_vec = left_tiles[:, :3, :, None] - right_tiles[:, :3, None, :]
    distance = jnp.sqrt(lax.optimization_barrier(jnp.sum(offset_vec * offset_vec, axis=1)) + SOFTENING)
    rad_left = left_tiles[:, 3, :, None]
    rad_right = right_tiles[:, 3, None, :]
    intersection = jnp.maximum(rad_left + rad_right - distance, 0.0)
    reduced = rad_left * rad_right / (rad_left + rad_right)
    magnitude = STIFFNESS * jnp.sqrt(reduced * intersection) * intersection / distance
    weighted = magnitude[:, None, :, :] * offset_vec
    return (lax.optimization_barrier(jnp.sum(weighted, axis=3)), -lax.optimization_barrier(jnp.sum(weighted, axis=2)))

def acceleration(force, radius):
    body_mass = 125.0 * radius * radius * radius
    gravity_term = jnp.zeros_like(force).at[:, 1, :].set(-0.5)
    return force / body_mass[:, None, :] + gravity_term

def device_forces(extended, neighbour_rows, live_count):
    own_bins = extended[GHOSTS:GHOSTS + BINS_DEV]
    self_force = lax.map(lambda inputs: pair_forces(inputs, inputs)[0], own_bins.reshape(BINS_DEV // BLOCK_TILES, BLOCK_TILES, 4, SPHERES))
    self_force = self_force.reshape(BINS_DEV, 3, SPHERES)
    flat_index = neighbour_rows.reshape(-1).astype(jnp.int32)
    left_tiles = jnp.repeat(own_bins, SLOTS, axis=0)
    right_tiles = jnp.take(extended, flat_index, axis=0)
    live_mask = (jnp.arange(SLOTS, dtype=jnp.int32)[None, :] < live_count[:, None]).reshape(-1).astype(extended.dtype)
    tile_blocks = BINS_DEV * SLOTS // BLOCK_TILES

    def block_forces(inputs):
        force_left, force_right = pair_forces(inputs[0], inputs[1])
        return (force_left * inputs[2][:, None, None], force_right * inputs[2][:, None, None])
    force_left, force_right = lax.map(block_forces, (left_tiles.reshape(tile_blocks, BLOCK_TILES, 4, SPHERES), right_tiles.reshape(tile_blocks, BLOCK_TILES, 4, SPHERES), live_mask.reshape(tile_blocks, BLOCK_TILES)))
    force_left = force_left.reshape(BINS_DEV, SLOTS, 3, SPHERES)
    force_right = force_right.reshape(BINS_DEV * SLOTS, 3 * SPHERES)
    candidate = BINS_DEV + 2 * GHOSTS
    onehot = (flat_index[:, None] == jnp.arange(candidate, dtype=jnp.int32)[None, :]).astype(extended.dtype)
    reaction = jnp.einsum('me,mf->ef', onehot, force_right, precision=lax.Precision.HIGHEST)
    reaction = reaction.reshape(candidate, 3, SPHERES)
    own_force = self_force + lax.optimization_barrier(jnp.sum(force_left, axis=1)) + reaction[GHOSTS:GHOSTS + BINS_DEV]
    return (own_force, reaction[:GHOSTS], reaction[GHOSTS + BINS_DEV:])

def reference(positions, radius, velocity, old_force, neighbours, tile_count):
    groups = N_SLAB * N_BLK
    accel_old = acceleration(old_force, radius)
    new_positions = positions + TIMESTEP * velocity + 0.5 * TIMESTEP * TIMESTEP * accel_old
    packed = jnp.concatenate([new_positions, radius[:, None, :]], axis=1)
    bin_grid = packed.reshape(N_SLAB, N_BLK, BINS_DEV, 4, SPHERES)
    empty_slab = jnp.zeros_like(bin_grid[:1])
    from_below = jnp.concatenate([empty_slab, bin_grid[:-1]], axis=0)[:, :, BINS_DEV - GHOSTS:]
    from_above = jnp.concatenate([bin_grid[1:], empty_slab], axis=0)[:, :, :GHOSTS]
    extended = jnp.concatenate([from_below, bin_grid, from_above], axis=2)
    extended = extended.reshape(groups, BINS_DEV + 2 * GHOSTS, 4, SPHERES)
    own_force, lower_part, upper_part = lax.map(lambda inputs: device_forces(inputs[0], inputs[1], inputs[2]), (extended, neighbours.reshape(groups, BINS_DEV, SLOTS), tile_count.reshape(groups, BINS_DEV)))
    own_force = own_force.reshape(N_SLAB, N_BLK, BINS_DEV, 3, SPHERES)
    lower_part = lower_part.reshape(N_SLAB, N_BLK, GHOSTS, 3, SPHERES)
    upper_part = upper_part.reshape(N_SLAB, N_BLK, GHOSTS, 3, SPHERES)
    own_force = own_force.at[:-1, :, BINS_DEV - GHOSTS:].add(lower_part[1:])
    own_force = own_force.at[1:, :, :GHOSTS].add(upper_part[:-1])
    new_force = own_force.reshape(N_SLAB * N_BLK * BINS_DEV, 3, SPHERES)
    new_velocity = velocity + 0.5 * TIMESTEP * (accel_old + acceleration(new_force, radius))
    return (new_positions, new_velocity, new_force)
```

```python
import functools

import jax
import jax.numpy as jnp
from jax import lax
from jax.experimental import pallas as pl
from jax.experimental.pallas import tpu as pltpu
from jax.sharding import PartitionSpec as P

GHOSTS = 8
STIFFNESS = 10.0
SOFTENING = 0.0025
TIMESTEP = 0.2
TINY = 1e-30
MESH = pl.DeviceIdType.MESH


def acceleration(force, radius):
    accel = force / (125.0 * radius * radius * radius)
    component = lax.broadcasted_iota(jnp.int32, accel.shape, 1)
    return accel + jnp.where(component == 1, -0.5, 0.0)


def greet(slabs, sectors):
    slab, sector = lax.axis_index("slab"), lax.axis_index("blk")
    barrier = pltpu.get_barrier_semaphore()
    for step in range(1, sectors):
        other = lax.rem(sector + step, sectors)
        pl.semaphore_signal(barrier, inc=1, device_id=(slab, other), device_id_type=MESH)

    @pl.when(slab > 0)
    def _():
        for step in range(sectors):
            other = lax.rem(sector + step, sectors)
            pl.semaphore_signal(barrier, inc=1, device_id=(slab - 1, other), device_id_type=MESH)

    @pl.when(slab < slabs - 1)
    def _():
        for step in range(sectors):
            other = lax.rem(sector + step, sectors)
            pl.semaphore_signal(barrier, inc=1, device_id=(slab + 1, other), device_id_type=MESH)

    beside = jnp.where(slab > 0, sectors, 0) + jnp.where(slab < slabs - 1, sectors, 0)
    pl.semaphore_wait(barrier, sectors - 1 + beside)


def spread_kernel(
    slabs, sectors, pos, rad, vel, old, neigh, count, ext, neigh_all, count_all, send, recv, local
):
    slab, sector = lax.axis_index("slab"), lax.axis_index("blk")
    bins = pos.shape[0]
    radius = rad[...][:, None, :]
    accel_old = acceleration(old[...], radius)
    moved = pos[...] + TIMESTEP * vel[...] + 0.5 * TIMESTEP * TIMESTEP * accel_old
    ext[sector, pl.ds(GHOSTS, bins), 0:3, :] = moved
    ext[sector, pl.ds(GHOSTS, bins), 3:4, :] = radius
    neigh_all[sector] = neigh[...]
    count_all[sector] = count[...]
    greet(slabs, sectors)

    def mate(step, what):
        other = lax.rem(sector + step, sectors)
        ref = (ext.at[sector, pl.ds(GHOSTS, bins)], neigh_all.at[sector], count_all.at[sector])[what]
        return pltpu.make_async_remote_copy(
            src_ref=ref, dst_ref=ref, send_sem=send.at[what, step], recv_sem=recv.at[what, step],
            device_id=(slab, other), device_id_type=MESH,
        )

    def beside(step, up):
        other = lax.rem(sector + step, sectors)
        own_first = bins if up else GHOSTS
        there = 0 if up else GHOSTS + bins
        return pltpu.make_async_remote_copy(
            src_ref=ext.at[sector, pl.ds(own_first, GHOSTS)],
            dst_ref=ext.at[sector, pl.ds(there, GHOSTS)],
            send_sem=send.at[3 + up, step], recv_sem=recv.at[3 + up, step],
            device_id=(slab + (1 if up else -1), other), device_id_type=MESH,
        )

    for step in range(1, sectors):
        for what in range(3):
            mate(step, what).start()

    @pl.when(slab > 0)
    def _():
        for step in range(sectors):
            beside(step, 0).start()

    @pl.when(slab < slabs - 1)
    def _():
        for step in range(sectors):
            beside(step, 1).start()

    for step in range(1, sectors):
        for what in range(3):
            mate(step, what).wait()

    @pl.when(slab > 0)
    def _():
        for step in range(sectors):
            beside(step, 0).wait_send()
            beside(step, 1).wait_recv()

    @pl.when(slab < slabs - 1)
    def _():
        for step in range(sectors):
            beside(step, 1).wait_send()
            beside(step, 0).wait_recv()


def tiles_kernel(sectors, neigh, count, ext, moved, react, acol, acc):
    sector = lax.axis_index("blk")
    bins = neigh.shape[1]
    spheres = ext.shape[3]
    moved[...] = ext[sector, pl.ds(GHOSTS, bins), 0:3, :]
    react[...] = jnp.zeros_like(react)
    total = lax.fori_loop(
        0, sectors * bins,
        lambda n, t: t + count[n // bins, 0, n % bins] + 1, 0, unroll=8,
    )
    first = total * sector // sectors
    last = total * (sector + 1) // sectors
    strips = spheres // 8

    def pair(other, both):
        row = [jnp.broadcast_to(other[c : c + 1, :], (8, spheres)) for c in range(4)]
        row.append(0.01 / row[3])
        total_b = [None] * 3
        for strip in range(strips):
            rows = pl.ds(8 * strip, 8)
            d = [acol[c, rows, :] - row[c] for c in range(3)]
            square = d[0] * d[0] + d[1] * d[1] + (d[2] * d[2] + SOFTENING)
            inverse = lax.rsqrt(square)
            overlap = jnp.maximum(acol[3, rows, :] + row[3] - square * inverse, TINY)
            stiff = lax.rsqrt(overlap * (acol[4, rows, :] + row[4]))
            pull = overlap * overlap * (inverse * stiff)
            for c in range(3):
                w = pull * d[c]
                total_b[c] = w if strip == 0 else total_b[c] + w
                if both:
                    acc[c, rows, :] += w
        return jnp.concatenate([jnp.sum(t, axis=0, keepdims=True) for t in total_b], axis=0)

    def one_bin(n, start):
        group, own = n // bins, n % bins
        units = count[group, 0, own] + 1
        low = jnp.maximum(first - start, 0)
        high = jnp.minimum(last - start, units)

        @pl.when(high > low)
        def _():
            mine = ext[group, GHOSTS + own]
            wide = jnp.concatenate([mine, 0.01 / mine], axis=0).T
            for c, column in enumerate((0, 1, 2, 3, 7)):
                acol[c] = jnp.broadcast_to(wide[:, column : column + 1], (spheres, spheres))
            acc[...] = jnp.zeros_like(acc)

            @pl.when(low == 0)
            def _():
                react[group, GHOSTS + own] -= pair(mine, False)

            def one_tile(k, _):
                candidate = neigh[group, own, k - 1]
                react[group, candidate] -= pair(ext[group, candidate], True)
                return 0

            lax.fori_loop(jnp.maximum(low, 1), high, one_tile, 0)
            rows = lax.dot_general(
                jnp.ones((8, spheres), jnp.float32), acc[...].reshape(3 * spheres, spheres),
                (((1,), (1,)), ((), ())), precision=lax.Precision.HIGHEST,
                preferred_element_type=jnp.float32,
            )
            react[group, GHOSTS + own] += jnp.concatenate(
                [rows[0:1, c * spheres : (c + 1) * spheres] for c in range(3)], axis=0
            )

        return start + units

    lax.fori_loop(0, sectors * bins, one_bin, 0)


def gather_kernel(slabs, sectors, bins, react, total, mates, below, above, send, recv):
    slab, sector = lax.axis_index("slab"), lax.axis_index("blk")
    greet(slabs, sectors)

    def mate(step):
        other = lax.rem(sector + step, sectors)
        return pltpu.make_async_remote_copy(
            src_ref=react.at[other, pl.ds(GHOSTS, bins)], dst_ref=mates.at[step],
            send_sem=send.at[0, step], recv_sem=recv.at[0, step],
            device_id=(slab, other), device_id_type=MESH,
        )

    def beside(step, up):
        other = lax.rem(sector + step, sectors)
        return pltpu.make_async_remote_copy(
            src_ref=react.at[other, pl.ds(GHOSTS + bins if up else 0, GHOSTS)],
            dst_ref=(below if up else above).at[step],
            send_sem=send.at[1 + up, step], recv_sem=recv.at[1 + up, step],
            device_id=(slab + (1 if up else -1), other), device_id_type=MESH,
        )

    for step in range(1, sectors):
        mate(step).start()

    @pl.when(slab > 0)
    def _():
        for step in range(sectors):
            beside(step, 0).start()

    @pl.when(slab < slabs - 1)
    def _():
        for step in range(sectors):
            beside(step, 1).start()

    total[...] = react[sector, pl.ds(GHOSTS, bins)]
    for step in range(1, sectors):
        mate(step).wait()
        total[...] += mates[step]

    @pl.when(slab > 0)
    def _():
        for step in range(sectors):
            beside(step, 0).wait_send()
            beside(step, 1).wait_recv()
            total[0:GHOSTS] += below[step]

    @pl.when(slab < slabs - 1)
    def _():
        for step in range(sectors):
            beside(step, 1).wait_send()
            beside(step, 0).wait_recv()
            total[pl.ds(bins - GHOSTS, GHOSTS)] += above[step]


def solution(mesh):
    slabs, sectors = mesh.shape["slab"], mesh.shape["blk"]
    vmem = pl.BlockSpec(memory_space=pltpu.VMEM)
    smem = pl.BlockSpec(memory_space=pltpu.SMEM)

    def local(positions, radius, velocity, old_force, neighbours, tile_count):
        bins, _, spheres = positions.shape
        slots = neighbours.shape[1]
        candidates = bins + 2 * GHOSTS
        ext, neigh_all, count_all = pl.pallas_call(
            functools.partial(spread_kernel, slabs, sectors),
            out_shape=(
                jax.ShapeDtypeStruct((sectors, candidates, 4, spheres), jnp.float32),
                jax.ShapeDtypeStruct((sectors, bins, slots), jnp.int32),
                jax.ShapeDtypeStruct((sectors, 1, bins), jnp.int32),
            ),
            in_specs=[vmem] * 6,
            out_specs=(vmem,) * 3,
            scratch_shapes=[
                pltpu.SemaphoreType.DMA((5, sectors)),
                pltpu.SemaphoreType.DMA((5, sectors)),
                pltpu.SemaphoreType.DMA((1,)),
            ],
            compiler_params=pltpu.CompilerParams(
                collective_id=0, has_side_effects=True, vmem_limit_bytes=32 * 2**20
            ),
        )(positions, radius, velocity, old_force, neighbours, tile_count.reshape(1, bins))
        moved, react = pl.pallas_call(
            functools.partial(tiles_kernel, sectors),
            out_shape=(
                jax.ShapeDtypeStruct((bins, 3, spheres), jnp.float32),
                jax.ShapeDtypeStruct((sectors, candidates, 3, spheres), jnp.float32),
            ),
            in_specs=[smem, smem, vmem],
            out_specs=(vmem, vmem),
            scratch_shapes=[
                pltpu.VMEM((5, spheres, spheres), jnp.float32),
                pltpu.VMEM((3, spheres, spheres), jnp.float32),
            ],
            compiler_params=pltpu.CompilerParams(vmem_limit_bytes=32 * 2**20),
        )(neigh_all, count_all, ext)
        force = pl.pallas_call(
            functools.partial(gather_kernel, slabs, sectors, bins),
            out_shape=jax.ShapeDtypeStruct((bins, 3, spheres), jnp.float32),
            in_specs=[vmem],
            out_specs=vmem,
            scratch_shapes=[
                pltpu.VMEM((sectors, bins, 3, spheres), jnp.float32),
                pltpu.VMEM((sectors, GHOSTS, 3, spheres), jnp.float32),
                pltpu.VMEM((sectors, GHOSTS, 3, spheres), jnp.float32),
                pltpu.SemaphoreType.DMA((3, sectors)),
                pltpu.SemaphoreType.DMA((3, sectors)),
            ],
            compiler_params=pltpu.CompilerParams(
                collective_id=1, has_side_effects=True, vmem_limit_bytes=32 * 2**20
            ),
        )(react)
        accel_sum = acceleration(old_force, radius[:, None, :]) + acceleration(force, radius[:, None, :])
        return (moved, velocity + 0.5 * TIMESTEP * accel_sum, force)

    spec = P(("slab", "blk"))
    return jax.shard_map(
        local, mesh=mesh, in_specs=(spec,) * 6, out_specs=(spec,) * 3, check_vma=False
    )
```

```python
import functools

import jax
import jax.numpy as jnp
from jax import lax
from jax.experimental import pallas as pl
from jax.experimental.pallas import tpu as pltpu
from jax.sharding import PartitionSpec as P

GHOSTS = 8
STIFFNESS = 10.0
SOFTENING = 0.0025
TIMESTEP = 0.2
TINY = 1e-30
BIN_COST = 3
MESH = pl.DeviceIdType.MESH


def acceleration(force, radius):
    accel = force / (125.0 * radius * radius * radius)
    component = lax.broadcasted_iota(jnp.int32, accel.shape, 1)
    return accel + jnp.where(component == 1, -0.5, 0.0)


def greet(slabs, sectors):
    slab, sector = lax.axis_index("slab"), lax.axis_index("blk")
    barrier = pltpu.get_barrier_semaphore()
    for step in range(1, sectors):
        other = lax.rem(sector + step, sectors)
        pl.semaphore_signal(barrier, inc=1, device_id=(slab, other), device_id_type=MESH)

    @pl.when(slab > 0)
    def _():
        for step in range(sectors):
            other = lax.rem(sector + step, sectors)
            pl.semaphore_signal(barrier, inc=1, device_id=(slab - 1, other), device_id_type=MESH)

    @pl.when(slab < slabs - 1)
    def _():
        for step in range(sectors):
            other = lax.rem(sector + step, sectors)
            pl.semaphore_signal(barrier, inc=1, device_id=(slab + 1, other), device_id_type=MESH)

    beside = jnp.where(slab > 0, sectors, 0) + jnp.where(slab < slabs - 1, sectors, 0)
    pl.semaphore_wait(barrier, sectors - 1 + beside)


def spread_kernel(
    slabs, sectors, pos_in, rad_in, vel_in, old_in, neigh_in, count_in,
    ext, neigh_all, count_all, base, mass, pos, rad, vel, old, send, recv, local,
):
    slab, sector = lax.axis_index("slab"), lax.axis_index("blk")
    bins = pos.shape[0]
    fetches = [
        pltpu.make_async_copy(source, target, local.at[index])
        for index, (source, target) in enumerate((
            (pos_in, pos), (rad_in, rad), (vel_in, vel), (old_in, old),
            (neigh_in, neigh_all.at[sector]), (count_in, count_all.at[sector]),
        ))
    ]
    for fetch in fetches:
        fetch.start()
    greet(slabs, sectors)
    for fetch in fetches:
        fetch.wait()
    radius = rad[...][:, None, :]
    accel_old = acceleration(old[...], radius)
    moved = pos[...] + TIMESTEP * vel[...] + 0.5 * TIMESTEP * TIMESTEP * accel_old
    ext[sector, pl.ds(GHOSTS, bins), 0:3, :] = moved
    ext[sector, pl.ds(GHOSTS, bins), 3:4, :] = radius

    def mate(step, what):
        other = lax.rem(sector + step, sectors)
        ref = (ext.at[sector, pl.ds(GHOSTS, bins)], neigh_all.at[sector], count_all.at[sector])[what]
        return pltpu.make_async_remote_copy(
            src_ref=ref, dst_ref=ref, send_sem=send.at[what, step], recv_sem=recv.at[what, step],
            device_id=(slab, other), device_id_type=MESH,
        )

    def beside(step, up):
        other = lax.rem(sector + step, sectors)
        own_first = bins if up else GHOSTS
        there = 0 if up else GHOSTS + bins
        return pltpu.make_async_remote_copy(
            src_ref=ext.at[sector, pl.ds(own_first, GHOSTS)],
            dst_ref=ext.at[sector, pl.ds(there, GHOSTS)],
            send_sem=send.at[3 + up, step], recv_sem=recv.at[3 + up, step],
            device_id=(slab + (1 if up else -1), other), device_id_type=MESH,
        )

    for step in range(1, sectors):
        for what in range(3):
            mate(step, what).start()

    @pl.when(slab > 0)
    def _():
        for step in range(sectors):
            beside(step, 0).start()

    @pl.when(slab < slabs - 1)
    def _():
        for step in range(sectors):
            beside(step, 1).start()

    base[...] = vel[...] + 0.5 * TIMESTEP * accel_old
    mass[...] = 125.0 * radius * radius * radius
    for step in range(1, sectors):
        for what in range(3):
            mate(step, what).wait()

    @pl.when(slab > 0)
    def _():
        for step in range(sectors):
            beside(step, 0).wait_send()
            beside(step, 1).wait_recv()

    @pl.when(slab < slabs - 1)
    def _():
        for step in range(sectors):
            beside(step, 1).wait_send()
            beside(step, 0).wait_recv()


def tiles_kernel(sectors, neigh, count, ext, moved_out, react, acol, acc, moved, done):
    sector = lax.axis_index("blk")
    bins = neigh.shape[1]
    spheres = ext.shape[3]
    strips = spheres // 8
    moved[...] = ext[sector, pl.ds(GHOSTS, bins), 0:3, :]
    store = pltpu.make_async_copy(moved, moved_out, done)
    store.start()
    react[...] = jnp.zeros_like(react)
    diagonal = lax.broadcasted_iota(jnp.int32, (spheres, spheres), 0) == lax.broadcasted_iota(
        jnp.int32, (spheres, spheres), 1
    )

    def group_units(group):
        return lax.fori_loop(
            0, bins, lambda own, t: t + count[group, 0, own] + BIN_COST, 0, unroll=bins
        )

    sizes = [group_units(group) for group in range(sectors)]
    total = sum(sizes)
    first = total * sector // sectors
    last = total * (sector + 1) // sectors

    def pair(others, both):
        rows_of = []
        for other in others:
            row = [jnp.broadcast_to(other[c : c + 1, :], (8, spheres)) for c in range(4)]
            rows_of.append(row + [0.01 / row[3]])
        totals = [[None] * 3 for _ in others]
        for strip in range(strips):
            rows = pl.ds(8 * strip, 8)
            column = [acol[c, rows, :] for c in range(5)]
            sums = [None] * 3
            for row, total_b in zip(rows_of, totals):
                d = [column[c] - row[c] for c in range(3)]
                square = d[0] * d[0] + d[1] * d[1] + (d[2] * d[2] + SOFTENING)
                inverse = lax.rsqrt(square)
                overlap = jnp.maximum(column[3] + row[3] - square * inverse, TINY)
                stiff = lax.rsqrt(overlap * (column[4] + row[4]))
                pull = overlap * overlap * (inverse * stiff)
                for c in range(3):
                    w = pull * d[c]
                    total_b[c] = w if strip == 0 else total_b[c] + w
                    sums[c] = w if sums[c] is None else sums[c] + w
            if both:
                for c in range(3):
                    acc[c, rows, :] += sums[c]
        return [
            jnp.concatenate([jnp.sum(t, axis=0, keepdims=True) for t in total_b], axis=0)
            for total_b in totals
        ]

    def one_bin(group, own, start):
        tiles = count[group, 0, own]
        units = tiles + BIN_COST
        low = jnp.maximum(first - start - BIN_COST, 0)
        high = jnp.minimum(last - start - BIN_COST, tiles)
        alone = (start >= first) & (start < last)

        @pl.when((high > low) | alone)
        def _():
            mine = ext[group, GHOSTS + own]
            wide = jnp.concatenate([mine, 0.01 / mine], axis=0).T
            for c, column in enumerate((0, 1, 2, 3, 7)):
                acol[c] = jnp.broadcast_to(wide[:, column : column + 1], (spheres, spheres))

            @pl.when(alone)
            def _():
                react[group, GHOSTS + own] -= pair([mine], False)[0]

            @pl.when(high > low)
            def _():
                acc[...] = jnp.zeros_like(acc)
                twos = (high - low) // 2

                def two_tiles(k, _):
                    one = neigh[group, own, low + 2 * k]
                    two = neigh[group, own, low + 2 * k + 1]
                    forces = pair([ext[group, one], ext[group, two]], True)
                    react[group, one] -= forces[0]
                    react[group, two] -= forces[1]
                    return 0

                lax.fori_loop(0, twos, two_tiles, 0)

                @pl.when(low + 2 * twos < high)
                def _():
                    one = neigh[group, own, high - 1]
                    react[group, one] -= pair([ext[group, one]], True)[0]

                react[group, GHOSTS + own] += jnp.concatenate(
                    [
                        jnp.sum(
                            jnp.where(diagonal, jnp.sum(acc[c], axis=1, keepdims=True), 0.0),
                            axis=0, keepdims=True,
                        )
                        for c in range(3)
                    ],
                    axis=0,
                )

        return start + units

    def one_group(group, start):
        stop = start
        for other in range(sectors):
            stop += jnp.where(group == other, sizes[other], 0)
        touched = (stop > first) & (start < last)
        lax.fori_loop(
            0, jnp.where(touched, bins, 0), functools.partial(one_bin, group), start
        )
        return stop

    lax.fori_loop(0, sectors, one_group, 0)
    store.wait()


def gather_kernel(slabs, sectors, bins, react, total, mates, below, above, send, recv):
    slab, sector = lax.axis_index("slab"), lax.axis_index("blk")
    greet(slabs, sectors)

    def mate(step):
        other = lax.rem(sector + step, sectors)
        return pltpu.make_async_remote_copy(
            src_ref=react.at[other, pl.ds(GHOSTS, bins)], dst_ref=mates.at[step],
            send_sem=send.at[0, step], recv_sem=recv.at[0, step],
            device_id=(slab, other), device_id_type=MESH,
        )

    def beside(step, up):
        other = lax.rem(sector + step, sectors)
        return pltpu.make_async_remote_copy(
            src_ref=react.at[other, pl.ds(GHOSTS + bins if up else 0, GHOSTS)],
            dst_ref=(below if up else above).at[step],
            send_sem=send.at[1 + up, step], recv_sem=recv.at[1 + up, step],
            device_id=(slab + (1 if up else -1), other), device_id_type=MESH,
        )

    for step in range(1, sectors):
        mate(step).start()

    @pl.when(slab > 0)
    def _():
        for step in range(sectors):
            beside(step, 0).start()

    @pl.when(slab < slabs - 1)
    def _():
        for step in range(sectors):
            beside(step, 1).start()

    total[...] = react[sector, pl.ds(GHOSTS, bins)]
    for step in range(1, sectors):
        mate(step).wait()
        total[...] += mates[step]

    @pl.when(slab > 0)
    def _():
        for step in range(sectors):
            beside(step, 0).wait_send()
            beside(step, 1).wait_recv()
            total[0:GHOSTS] += below[step]

    @pl.when(slab < slabs - 1)
    def _():
        for step in range(sectors):
            beside(step, 1).wait_send()
            beside(step, 0).wait_recv()
            total[pl.ds(bins - GHOSTS, GHOSTS)] += above[step]


def finish_kernel(force, base, mass, velocity_out, force_out, velocity, done):
    copy_force = pltpu.make_async_copy(force, force_out, done.at[0])
    copy_force.start()
    component = lax.broadcasted_iota(jnp.int32, force.shape, 1)
    accel = force[...] / mass[...] + jnp.where(component == 1, -0.5, 0.0)
    velocity[...] = base[...] + 0.5 * TIMESTEP * accel
    copy_velocity = pltpu.make_async_copy(velocity, velocity_out, done.at[1])
    copy_velocity.start()
    copy_force.wait()
    copy_velocity.wait()


def solution(mesh):
    slabs, sectors = mesh.shape["slab"], mesh.shape["blk"]
    vmem = pl.BlockSpec(memory_space=pltpu.VMEM)
    smem = pl.BlockSpec(memory_space=pltpu.SMEM)
    hbm = pl.BlockSpec(memory_space=pltpu.HBM)

    def local(positions, radius, velocity, old_force, neighbours, tile_count):
        bins, _, spheres = positions.shape
        slots = neighbours.shape[1]
        candidates = bins + 2 * GHOSTS
        ext, neigh_all, count_all, base, mass = pl.pallas_call(
            functools.partial(spread_kernel, slabs, sectors),
            out_shape=(
                jax.ShapeDtypeStruct((sectors, candidates, 4, spheres), jnp.float32),
                jax.ShapeDtypeStruct((sectors, bins, slots), jnp.int32),
                jax.ShapeDtypeStruct((sectors, 1, bins), jnp.int32),
                jax.ShapeDtypeStruct((bins, 3, spheres), jnp.float32),
                jax.ShapeDtypeStruct((bins, 1, spheres), jnp.float32),
            ),
            in_specs=[hbm] * 6,
            out_specs=(vmem,) * 5,
            scratch_shapes=[
                pltpu.VMEM((bins, 3, spheres), jnp.float32),
                pltpu.VMEM((bins, spheres), jnp.float32),
                pltpu.VMEM((bins, 3, spheres), jnp.float32),
                pltpu.VMEM((bins, 3, spheres), jnp.float32),
                pltpu.SemaphoreType.DMA((5, sectors)),
                pltpu.SemaphoreType.DMA((5, sectors)),
                pltpu.SemaphoreType.DMA((6,)),
            ],
            compiler_params=pltpu.CompilerParams(
                collective_id=0, has_side_effects=True, vmem_limit_bytes=32 * 2**20
            ),
        )(positions, radius, velocity, old_force, neighbours, tile_count.reshape(1, bins))
        moved, react = pl.pallas_call(
            functools.partial(tiles_kernel, sectors),
            out_shape=(
                jax.ShapeDtypeStruct((bins, 3, spheres), jnp.float32),
                jax.ShapeDtypeStruct((sectors, candidates, 3, spheres), jnp.float32),
            ),
            in_specs=[smem, smem, vmem],
            out_specs=(hbm, vmem),
            scratch_shapes=[
                pltpu.VMEM((5, spheres, spheres), jnp.float32),
                pltpu.VMEM((3, spheres, spheres), jnp.float32),
                pltpu.VMEM((bins, 3, spheres), jnp.float32),
                pltpu.SemaphoreType.DMA,
            ],
            compiler_params=pltpu.CompilerParams(vmem_limit_bytes=32 * 2**20),
        )(neigh_all, count_all, ext)
        force = pl.pallas_call(
            functools.partial(gather_kernel, slabs, sectors, bins),
            out_shape=jax.ShapeDtypeStruct((bins, 3, spheres), jnp.float32),
            in_specs=[vmem],
            out_specs=vmem,
            scratch_shapes=[
                pltpu.VMEM((sectors, bins, 3, spheres), jnp.float32),
                pltpu.VMEM((sectors, GHOSTS, 3, spheres), jnp.float32),
                pltpu.VMEM((sectors, GHOSTS, 3, spheres), jnp.float32),
                pltpu.SemaphoreType.DMA((3, sectors)),
                pltpu.SemaphoreType.DMA((3, sectors)),
            ],
            compiler_params=pltpu.CompilerParams(
                collective_id=1, has_side_effects=True, vmem_limit_bytes=32 * 2**20
            ),
        )(react)
        velocity_new, force_new = pl.pallas_call(
            finish_kernel,
            out_shape=(jax.ShapeDtypeStruct((bins, 3, spheres), jnp.float32),) * 2,
            in_specs=[vmem] * 3,
            out_specs=(hbm, hbm),
            scratch_shapes=[
                pltpu.VMEM((bins, 3, spheres), jnp.float32),
                pltpu.SemaphoreType.DMA((2,)),
            ],
        )(force, base, mass)
        return (moved, velocity_new, force_new)

    spec = P(("slab", "blk"))
    return jax.shard_map(
        local, mesh=mesh, in_specs=(spec,) * 6, out_specs=(spec,) * 3, check_vma=False
    )
```

```python
import functools

import jax
import jax.numpy as jnp
from jax import lax
from jax.experimental import pallas as pl
from jax.experimental.pallas import tpu as pltpu
from jax.sharding import PartitionSpec as P

GHOSTS = 8
STIFFNESS = 10.0
SOFTENING = 0.0025
TIMESTEP = 0.2
TINY = 1e-30
BIN_COST = 3
MESH = pl.DeviceIdType.MESH


def acceleration(force, mass, component):
    accel = force / mass
    return accel - 0.5 if component == 1 else accel


def greet(slabs, sectors):
    slab, sector = lax.axis_index("slab"), lax.axis_index("blk")
    barrier = pltpu.get_barrier_semaphore()
    for step in range(1, sectors):
        other = lax.rem(sector + step, sectors)
        pl.semaphore_signal(barrier, inc=1, device_id=(slab, other), device_id_type=MESH)

    @pl.when(slab > 0)
    def _():
        for step in range(sectors):
            other = lax.rem(sector + step, sectors)
            pl.semaphore_signal(barrier, inc=1, device_id=(slab - 1, other), device_id_type=MESH)

    @pl.when(slab < slabs - 1)
    def _():
        for step in range(sectors):
            other = lax.rem(sector + step, sectors)
            pl.semaphore_signal(barrier, inc=1, device_id=(slab + 1, other), device_id_type=MESH)

    beside = jnp.where(slab > 0, sectors, 0) + jnp.where(slab < slabs - 1, sectors, 0)
    pl.semaphore_wait(barrier, sectors - 1 + beside)


def spread_kernel(
    slabs, sectors, pos_in, rad_in, vel_in, old_in, neigh_in, count_in,
    ext, neigh_all, count_all, base, mass, pos, rad, vel, old, send, recv, local,
):
    slab, sector = lax.axis_index("slab"), lax.axis_index("blk")
    bins = pos.shape[1]
    fetches = [
        pltpu.make_async_copy(source, target, local.at[index])
        for index, (source, target) in enumerate((
            (pos_in, pos), (rad_in, rad), (vel_in, vel), (old_in, old),
            (neigh_in, neigh_all.at[sector]), (count_in, count_all.at[sector]),
        ))
    ]
    for fetch in fetches:
        fetch.start()
    greet(slabs, sectors)
    for fetch in fetches:
        fetch.wait()
    radius = rad[...]
    mass[...] = 125.0 * radius * radius * radius
    accel_old = [acceleration(old[c], mass[...], c) for c in range(3)]
    for c in range(3):
        moved = pos[c] + TIMESTEP * vel[c] + 0.5 * TIMESTEP * TIMESTEP * accel_old[c]
        ext[sector, pl.ds(GHOSTS, bins), c : c + 1, :] = moved[:, None, :]
    ext[sector, pl.ds(GHOSTS, bins), 3:4, :] = radius[:, None, :]

    def mate(step, what):
        other = lax.rem(sector + step, sectors)
        ref = (ext.at[sector, pl.ds(GHOSTS, bins)], neigh_all.at[sector], count_all.at[sector])[what]
        return pltpu.make_async_remote_copy(
            src_ref=ref, dst_ref=ref, send_sem=send.at[what, step], recv_sem=recv.at[what, step],
            device_id=(slab, other), device_id_type=MESH,
        )

    def beside(step, up):
        other = lax.rem(sector + step, sectors)
        own_first = bins if up else GHOSTS
        there = 0 if up else GHOSTS + bins
        return pltpu.make_async_remote_copy(
            src_ref=ext.at[sector, pl.ds(own_first, GHOSTS)],
            dst_ref=ext.at[sector, pl.ds(there, GHOSTS)],
            send_sem=send.at[3 + up, step], recv_sem=recv.at[3 + up, step],
            device_id=(slab + (1 if up else -1), other), device_id_type=MESH,
        )

    for step in range(1, sectors):
        for what in range(3):
            mate(step, what).start()

    @pl.when(slab > 0)
    def _():
        for step in range(sectors):
            beside(step, 0).start()

    @pl.when(slab < slabs - 1)
    def _():
        for step in range(sectors):
            beside(step, 1).start()

    for c in range(3):
        base[c] = vel[c] + 0.5 * TIMESTEP * accel_old[c]
    for step in range(1, sectors):
        for what in range(3):
            mate(step, what).wait()

    @pl.when(slab > 0)
    def _():
        for step in range(sectors):
            beside(step, 0).wait_send()
            beside(step, 1).wait_recv()

    @pl.when(slab < slabs - 1)
    def _():
        for step in range(sectors):
            beside(step, 1).wait_send()
            beside(step, 0).wait_recv()


def tiles_kernel(sectors, neigh, count, ext, moved_out, react, acol, acc, select, moved, done):
    sector = lax.axis_index("blk")
    bins = neigh.shape[2]
    spheres = ext.shape[3]
    strips = spheres // 8
    spare = bins + 2 * GHOSTS
    for c in range(3):
        moved[c] = ext[sector, pl.ds(GHOSTS, bins), c, :]
    store = pltpu.make_async_copy(moved, moved_out, done)
    store.start()
    react[...] = jnp.zeros_like(react)
    diagonal = lax.broadcasted_iota(jnp.int32, (spheres, spheres), 0) == lax.broadcasted_iota(
        jnp.int32, (spheres, spheres), 1
    )
    piece = lax.broadcasted_iota(jnp.int32, select.shape, 0)
    block = lax.broadcasted_iota(jnp.int32, select.shape, 1) // spheres
    wanted = jnp.where(block == 4, 7, block)
    select[...] = jnp.where(piece % 8 == wanted, 1.0, 0.0).astype(jnp.bfloat16)
    ones = jnp.ones((2 * spheres, spheres), jnp.bfloat16)

    def fill_columns(mine):
        wide = jnp.concatenate([mine, 0.01 / mine[3:4], 0.01 / mine[3:4], 0.01 / mine[3:4], 0.01 / mine[3:4]], axis=0)
        top = wide.astype(jnp.bfloat16).astype(jnp.float32)
        middle = (wide - top).astype(jnp.bfloat16).astype(jnp.float32)
        low = wide - top - middle
        pieces = jnp.concatenate([top, middle, low, jnp.zeros_like(low)], axis=0).T
        acol[...] = jnp.dot(
            pieces.astype(jnp.bfloat16), select[...], preferred_element_type=jnp.float32
        )

    def row_sums():
        whole = acc[...].reshape(3 * spheres, spheres)
        top = whole.astype(jnp.bfloat16)
        rest = (whole - top.astype(jnp.float32)).astype(jnp.bfloat16)
        sums = jnp.dot(
            jnp.concatenate([top, rest], axis=1), ones, preferred_element_type=jnp.float32
        )
        return jnp.concatenate(
            [
                jnp.sum(
                    jnp.where(diagonal, sums[c * spheres : (c + 1) * spheres], 0.0),
                    axis=0, keepdims=True,
                )
                for c in range(3)
            ],
            axis=0,
        )

    def group_units(group):
        return lax.fori_loop(
            0, bins, lambda own, t: t + count[group, 0, own] + 1 + BIN_COST, 0, unroll=bins
        )

    sizes = [group_units(group) for group in range(sectors)]
    total = sum(sizes)
    first = total * sector // sectors
    last = total * (sector + 1) // sectors

    def pair(others):
        rows_of = []
        for other in others:
            row = [jnp.broadcast_to(other[c : c + 1, :], (8, spheres)) for c in range(4)]
            rows_of.append(row + [0.01 / row[3]])
        totals = [[None] * 3 for _ in others]
        for strip in range(strips):
            rows = pl.ds(8 * strip, 8)
            column = [acol[rows, c * spheres : (c + 1) * spheres] for c in range(5)]
            sums = [None] * 3
            for row, total_b in zip(rows_of, totals):
                d = [column[c] - row[c] for c in range(3)]
                square = d[0] * d[0] + d[1] * d[1] + (d[2] * d[2] + SOFTENING)
                inverse = lax.rsqrt(square)
                overlap = jnp.maximum(column[3] + row[3] - square * inverse, TINY)
                stiff = lax.rsqrt(overlap * (column[4] + row[4]))
                pull = overlap * overlap * (inverse * stiff)
                for c in range(3):
                    w = pull * d[c]
                    total_b[c] = w if strip == 0 else total_b[c] + w
                    sums[c] = w if sums[c] is None else sums[c] + w
            for c in range(3):
                acc[c, rows, :] += sums[c]
        return [
            jnp.concatenate([jnp.sum(t, axis=0, keepdims=True) for t in total_b], axis=0)
            for total_b in totals
        ]

    def one_bin(group, own, start):
        tiles = count[group, 0, own] + 1
        low = jnp.maximum(first - start - BIN_COST, 0)
        high = jnp.minimum(last - start - BIN_COST, tiles)

        def unit(k):
            other = neigh[group, jnp.maximum(k - 1, 0), own]
            return jnp.where(k == 0, GHOSTS + own, other), jnp.where(k == 0, spare, other)

        @pl.when(high > low)
        def _():
            fill_columns(ext[group, GHOSTS + own])
            acc[...] = jnp.zeros_like(acc)
            twos = (high - low) // 2

            def two_tiles(k, _):
                (one, to_one), (two, to_two) = unit(low + 2 * k), unit(low + 2 * k + 1)
                forces = pair([ext[group, one], ext[group, two]])
                react[group, to_one] -= forces[0]
                react[group, to_two] -= forces[1]
                return 0

            lax.fori_loop(0, twos, two_tiles, 0)

            @pl.when(low + 2 * twos < high)
            def _():
                one, to_one = unit(high - 1)
                react[group, to_one] -= pair([ext[group, one]])[0]

            react[group, GHOSTS + own] += row_sums()

        return start + tiles + BIN_COST

    def one_group(group, start):
        stop = start
        for other in range(sectors):
            stop += jnp.where(group == other, sizes[other], 0)
        touched = (stop > first) & (start < last)
        lax.fori_loop(
            0, jnp.where(touched, bins, 0), functools.partial(one_bin, group), start
        )
        return stop

    lax.fori_loop(0, sectors, one_group, 0)
    store.wait()


def gather_kernel(slabs, sectors, bins, react, total, mates, below, above, send, recv):
    slab, sector = lax.axis_index("slab"), lax.axis_index("blk")
    greet(slabs, sectors)

    def mate(step):
        other = lax.rem(sector + step, sectors)
        return pltpu.make_async_remote_copy(
            src_ref=react.at[other, pl.ds(GHOSTS, bins)], dst_ref=mates.at[step],
            send_sem=send.at[0, step], recv_sem=recv.at[0, step],
            device_id=(slab, other), device_id_type=MESH,
        )

    def beside(step, up):
        other = lax.rem(sector + step, sectors)
        return pltpu.make_async_remote_copy(
            src_ref=react.at[other, pl.ds(GHOSTS + bins if up else 0, GHOSTS)],
            dst_ref=(below if up else above).at[step],
            send_sem=send.at[1 + up, step], recv_sem=recv.at[1 + up, step],
            device_id=(slab + (1 if up else -1), other), device_id_type=MESH,
        )

    for step in range(1, sectors):
        mate(step).start()

    @pl.when(slab > 0)
    def _():
        for step in range(sectors):
            beside(step, 0).start()

    @pl.when(slab < slabs - 1)
    def _():
        for step in range(sectors):
            beside(step, 1).start()

    total[...] = react[sector, pl.ds(GHOSTS, bins)]
    for step in range(1, sectors):
        mate(step).wait()
        total[...] += mates[step]

    @pl.when(slab > 0)
    def _():
        for step in range(sectors):
            beside(step, 0).wait_send()
            beside(step, 1).wait_recv()
            total[0:GHOSTS] += below[step]

    @pl.when(slab < slabs - 1)
    def _():
        for step in range(sectors):
            beside(step, 1).wait_send()
            beside(step, 0).wait_recv()
            total[pl.ds(bins - GHOSTS, GHOSTS)] += above[step]


def finish_kernel(force, base, mass, velocity_out, force_out, velocity, turned, done):
    for c in range(3):
        turned[c] = force[:, c, :]
    copy_force = pltpu.make_async_copy(turned, force_out, done.at[0])
    copy_force.start()
    for c in range(3):
        velocity[c] = base[c] + 0.5 * TIMESTEP * acceleration(turned[c], mass[...], c)
    copy_velocity = pltpu.make_async_copy(velocity, velocity_out, done.at[1])
    copy_velocity.start()
    copy_force.wait()
    copy_velocity.wait()


def solution(mesh):
    slabs, sectors = mesh.shape["slab"], mesh.shape["blk"]
    vmem = pl.BlockSpec(memory_space=pltpu.VMEM)
    smem = pl.BlockSpec(memory_space=pltpu.SMEM)
    hbm = pl.BlockSpec(memory_space=pltpu.HBM)

    def local(positions, radius, velocity, old_force, neighbours, tile_count):
        bins, _, spheres = positions.shape
        first_axis = lambda array: jnp.transpose(array, (1, 0, 2))
        slots = neighbours.shape[1]
        candidates = bins + 2 * GHOSTS
        ext, neigh_all, count_all, base, mass = pl.pallas_call(
            functools.partial(spread_kernel, slabs, sectors),
            out_shape=(
                jax.ShapeDtypeStruct((sectors, candidates, 4, spheres), jnp.float32),
                jax.ShapeDtypeStruct((sectors, slots, bins), jnp.int32),
                jax.ShapeDtypeStruct((sectors, 1, bins), jnp.int32),
                jax.ShapeDtypeStruct((3, bins, spheres), jnp.float32),
                jax.ShapeDtypeStruct((bins, spheres), jnp.float32),
            ),
            in_specs=[hbm] * 6,
            out_specs=(vmem,) * 5,
            scratch_shapes=[
                pltpu.VMEM((3, bins, spheres), jnp.float32),
                pltpu.VMEM((bins, spheres), jnp.float32),
                pltpu.VMEM((3, bins, spheres), jnp.float32),
                pltpu.VMEM((3, bins, spheres), jnp.float32),
                pltpu.SemaphoreType.DMA((5, sectors)),
                pltpu.SemaphoreType.DMA((5, sectors)),
                pltpu.SemaphoreType.DMA((6,)),
            ],
            compiler_params=pltpu.CompilerParams(
                collective_id=0, has_side_effects=True, vmem_limit_bytes=8 * 2**20
            ),
        )(
            first_axis(positions), radius, first_axis(velocity), first_axis(old_force),
            neighbours.T, tile_count.reshape(1, bins),
        )
        moved, react = pl.pallas_call(
            functools.partial(tiles_kernel, sectors),
            out_shape=(
                jax.ShapeDtypeStruct((3, bins, spheres), jnp.float32),
                jax.ShapeDtypeStruct((sectors, candidates + 1, 3, spheres), jnp.float32),
            ),
            in_specs=[smem, smem, vmem],
            out_specs=(hbm, vmem),
            scratch_shapes=[
                pltpu.VMEM((spheres, 5 * spheres), jnp.float32),
                pltpu.VMEM((3, spheres, spheres), jnp.float32),
                pltpu.VMEM((32, 5 * spheres), jnp.bfloat16),
                pltpu.VMEM((3, bins, spheres), jnp.float32),
                pltpu.SemaphoreType.DMA,
            ],
            compiler_params=pltpu.CompilerParams(vmem_limit_bytes=8 * 2**20),
        )(neigh_all, count_all, ext)
        force = pl.pallas_call(
            functools.partial(gather_kernel, slabs, sectors, bins),
            out_shape=jax.ShapeDtypeStruct((bins, 3, spheres), jnp.float32),
            in_specs=[vmem],
            out_specs=vmem,
            scratch_shapes=[
                pltpu.VMEM((sectors, bins, 3, spheres), jnp.float32),
                pltpu.VMEM((sectors, GHOSTS, 3, spheres), jnp.float32),
                pltpu.VMEM((sectors, GHOSTS, 3, spheres), jnp.float32),
                pltpu.SemaphoreType.DMA((3, sectors)),
                pltpu.SemaphoreType.DMA((3, sectors)),
            ],
            compiler_params=pltpu.CompilerParams(
                collective_id=1, has_side_effects=True, vmem_limit_bytes=8 * 2**20
            ),
        )(react)
        velocity_new, force_new = pl.pallas_call(
            finish_kernel,
            out_shape=(jax.ShapeDtypeStruct((3, bins, spheres), jnp.float32),) * 2,
            in_specs=[vmem] * 3,
            out_specs=(hbm, hbm),
            scratch_shapes=[
                pltpu.VMEM((3, bins, spheres), jnp.float32),
                pltpu.VMEM((3, bins, spheres), jnp.float32),
                pltpu.SemaphoreType.DMA((2,)),
            ],
            compiler_params=pltpu.CompilerParams(vmem_limit_bytes=8 * 2**20),
        )(force, base, mass)
        return (first_axis(moved), first_axis(velocity_new), first_axis(force_new))

    spec = P(("slab", "blk"))
    return jax.shard_map(
        local, mesh=mesh, in_specs=(spec,) * 6, out_specs=(spec,) * 3, check_vma=False
    )
```

```python
import functools

import jax
import jax.numpy as jnp
from jax import lax
from jax.experimental import pallas as pl
from jax.experimental.pallas import tpu as pltpu
from jax.sharding import PartitionSpec as P

GHOSTS = 8
STIFFNESS = 10.0
SOFTENING = 0.0025
TIMESTEP = 0.2
TINY = 1e-30
BIN_COST = 3
CHUNK = 4
MESH = pl.DeviceIdType.MESH


def acceleration(force, mass, component):
    accel = force / mass
    return accel - 0.5 if component == 1 else accel


def greet(slabs, sectors):
    slab, sector = lax.axis_index("slab"), lax.axis_index("blk")
    barrier = pltpu.get_barrier_semaphore()
    for step in range(1, sectors):
        other = lax.rem(sector + step, sectors)
        pl.semaphore_signal(barrier, inc=1, device_id=(slab, other), device_id_type=MESH)

    @pl.when(slab > 0)
    def _():
        for step in range(sectors):
            other = lax.rem(sector + step, sectors)
            pl.semaphore_signal(barrier, inc=1, device_id=(slab - 1, other), device_id_type=MESH)

    @pl.when(slab < slabs - 1)
    def _():
        for step in range(sectors):
            other = lax.rem(sector + step, sectors)
            pl.semaphore_signal(barrier, inc=1, device_id=(slab + 1, other), device_id_type=MESH)

    beside = jnp.where(slab > 0, sectors, 0) + jnp.where(slab < slabs - 1, sectors, 0)
    pl.semaphore_wait(barrier, sectors - 1 + beside)


def spread_kernel(
    slabs, sectors, pos_in, rad_in, vel_in, old_in, neigh_in, count_in,
    ext, neigh_all, count_all, base, mass, pos, rad, vel, old, send, recv, local,
):
    slab, sector = lax.axis_index("slab"), lax.axis_index("blk")
    bins = pos.shape[1]
    fetches = [
        pltpu.make_async_copy(source, target, local.at[index])
        for index, (source, target) in enumerate((
            (pos_in, pos), (rad_in, rad), (vel_in, vel), (old_in, old),
            (neigh_in, neigh_all.at[sector]), (count_in, count_all.at[sector]),
        ))
    ]
    for fetch in fetches:
        fetch.start()
    greet(slabs, sectors)
    for fetch in fetches:
        fetch.wait()
    radius = rad[...]
    mass[...] = 125.0 * radius * radius * radius
    accel_old = [acceleration(old[c], mass[...], c) for c in range(3)]
    for c in range(3):
        moved = pos[c] + TIMESTEP * vel[c] + 0.5 * TIMESTEP * TIMESTEP * accel_old[c]
        ext[sector, pl.ds(GHOSTS, bins), c : c + 1, :] = moved[:, None, :]
    ext[sector, pl.ds(GHOSTS, bins), 3:4, :] = radius[:, None, :]

    def mate(step, what):
        other = lax.rem(sector + step, sectors)
        ref = (ext.at[sector, pl.ds(GHOSTS, bins)], neigh_all.at[sector], count_all.at[sector])[what]
        return pltpu.make_async_remote_copy(
            src_ref=ref, dst_ref=ref, send_sem=send.at[what, step], recv_sem=recv.at[what, step],
            device_id=(slab, other), device_id_type=MESH,
        )

    def beside(step, up):
        other = lax.rem(sector + step, sectors)
        own_first = bins if up else GHOSTS
        there = 0 if up else GHOSTS + bins
        return pltpu.make_async_remote_copy(
            src_ref=ext.at[sector, pl.ds(own_first, GHOSTS)],
            dst_ref=ext.at[sector, pl.ds(there, GHOSTS)],
            send_sem=send.at[3 + up, step], recv_sem=recv.at[3 + up, step],
            device_id=(slab + (1 if up else -1), other), device_id_type=MESH,
        )

    for step in range(1, sectors):
        for what in range(3):
            mate(step, what).start()

    @pl.when(slab > 0)
    def _():
        for step in range(sectors):
            beside(step, 0).start()

    @pl.when(slab < slabs - 1)
    def _():
        for step in range(sectors):
            beside(step, 1).start()

    for c in range(3):
        base[c] = vel[c] + 0.5 * TIMESTEP * accel_old[c]
    for step in range(1, sectors):
        for what in range(3):
            mate(step, what).wait()

    @pl.when(slab > 0)
    def _():
        for step in range(sectors):
            beside(step, 0).wait_send()
            beside(step, 1).wait_recv()

    @pl.when(slab < slabs - 1)
    def _():
        for step in range(sectors):
            beside(step, 1).wait_send()
            beside(step, 0).wait_recv()


def tiles_kernel(sectors, neigh, count, ext, moved_out, react, acol, acc, moved, done):
    sector = lax.axis_index("blk")
    bins = neigh.shape[2]
    spheres = ext.shape[3]
    strips = spheres // 8
    spare = bins + 2 * GHOSTS
    for c in range(3):
        moved[c] = ext[sector, pl.ds(GHOSTS, bins), c, :]
    store = pltpu.make_async_copy(moved, moved_out, done)
    store.start()
    react[...] = jnp.zeros_like(react)
    diagonal = lax.broadcasted_iota(jnp.int32, (spheres, spheres), 0) == lax.broadcasted_iota(
        jnp.int32, (spheres, spheres), 1
    )

    def fill_columns(slot, mine):
        wide = jnp.concatenate([mine, 0.01 / mine], axis=0).T
        for c, column in enumerate((0, 1, 2, 3, 7)):
            acol[slot, c] = jnp.broadcast_to(wide[:, column : column + 1], (spheres, spheres))
        acc[slot] = jnp.zeros((3, spheres, spheres), jnp.float32)

    def row_sums(slot):
        return jnp.concatenate(
            [
                jnp.sum(
                    jnp.where(diagonal, jnp.sum(acc[slot, c], axis=1, keepdims=True), 0.0),
                    axis=0, keepdims=True,
                )
                for c in range(3)
            ],
            axis=0,
        )

    def group_units(group):
        return lax.fori_loop(
            0, bins, lambda own, t: t + count[group, 0, own] + 1 + BIN_COST, 0, unroll=bins
        )

    sizes = [group_units(group) for group in range(sectors)]
    total = sum(sizes)
    first = total * sector // sectors
    last = total * (sector + 1) // sectors

    def pair(slot, others):
        rows_of = []
        for other in others:
            row = [jnp.broadcast_to(other[c : c + 1, :], (8, spheres)) for c in range(4)]
            rows_of.append(row + [0.01 / row[3]])
        totals = [[None] * 3 for _ in others]
        for strip in range(strips):
            rows = pl.ds(8 * strip, 8)
            column = [acol[slot, c, rows, :] for c in range(5)]
            sums = [None] * 3
            for row, total_b in zip(rows_of, totals):
                d = [column[c] - row[c] for c in range(3)]
                square = d[0] * d[0] + d[1] * d[1] + (d[2] * d[2] + SOFTENING)
                inverse = lax.rsqrt(square)
                overlap = jnp.maximum(column[3] + row[3] - square * inverse, TINY)
                stiff = lax.rsqrt(overlap * (column[4] + row[4]))
                pull = overlap * overlap * (inverse * stiff)
                for c in range(3):
                    w = pull * d[c]
                    total_b[c] = w if strip == 0 else total_b[c] + w
                    sums[c] = w if sums[c] is None else sums[c] + w
            for c in range(3):
                acc[slot, c, rows, :] += sums[c]
        return [
            jnp.concatenate([jnp.sum(t, axis=0, keepdims=True) for t in total_b], axis=0)
            for total_b in totals
        ]

    def one_bin(group, chunk, slot, start):
        own = chunk * CHUNK + slot
        tiles = count[group, 0, own] + 1
        low = jnp.maximum(first - start - BIN_COST, 0)
        high = jnp.maximum(jnp.minimum(last - start - BIN_COST, tiles), low)

        def unit(k):
            other = neigh[group, jnp.maximum(k - 1, 0), own]
            return jnp.where(k == 0, GHOSTS + own, other), jnp.where(k == 0, spare, other)

        twos = (high - low) // 2

        def two_tiles(k, _):
            (one, to_one), (two, to_two) = unit(low + 2 * k), unit(low + 2 * k + 1)
            forces = pair(slot, [ext[group, one], ext[group, two]])
            react[group, to_one] -= forces[0]
            react[group, to_two] -= forces[1]
            return 0

        lax.fori_loop(0, twos, two_tiles, 0)

        @pl.when(low + 2 * twos < high)
        def _():
            one, to_one = unit(high - 1)
            react[group, to_one] -= pair(slot, [ext[group, one]])[0]

        return start + tiles + BIN_COST

    def one_chunk(group, chunk, start):
        stop = start
        for slot in range(CHUNK):
            stop += count[group, 0, chunk * CHUNK + slot] + 1 + BIN_COST

        @pl.when((stop > first) & (start < last))
        def _():
            here = GHOSTS + chunk * CHUNK
            for slot in range(CHUNK):
                fill_columns(slot, ext[group, here + slot])
            lax.fori_loop(0, CHUNK, functools.partial(one_bin, group, chunk), start)
            sums = [row_sums(slot) for slot in range(CHUNK)]
            for slot in range(CHUNK):
                react[group, here + slot] += sums[slot]

        return stop

    def one_group(group, start):
        stop = start
        for other in range(sectors):
            stop += jnp.where(group == other, sizes[other], 0)
        touched = (stop > first) & (start < last)
        lax.fori_loop(
            0, jnp.where(touched, bins // CHUNK, 0), functools.partial(one_chunk, group), start
        )
        return stop

    lax.fori_loop(0, sectors, one_group, 0)
    store.wait()


def gather_kernel(slabs, sectors, bins, react, total, mates, below, above, send, recv):
    slab, sector = lax.axis_index("slab"), lax.axis_index("blk")
    greet(slabs, sectors)

    def mate(step):
        other = lax.rem(sector + step, sectors)
        return pltpu.make_async_remote_copy(
            src_ref=react.at[other, pl.ds(GHOSTS, bins)], dst_ref=mates.at[step],
            send_sem=send.at[0, step], recv_sem=recv.at[0, step],
            device_id=(slab, other), device_id_type=MESH,
        )

    def beside(step, up):
        other = lax.rem(sector + step, sectors)
        return pltpu.make_async_remote_copy(
            src_ref=react.at[other, pl.ds(GHOSTS + bins if up else 0, GHOSTS)],
            dst_ref=(below if up else above).at[step],
            send_sem=send.at[1 + up, step], recv_sem=recv.at[1 + up, step],
            device_id=(slab + (1 if up else -1), other), device_id_type=MESH,
        )

    for step in range(1, sectors):
        mate(step).start()

    @pl.when(slab > 0)
    def _():
        for step in range(sectors):
            beside(step, 0).start()

    @pl.when(slab < slabs - 1)
    def _():
        for step in range(sectors):
            beside(step, 1).start()

    total[...] = react[sector, pl.ds(GHOSTS, bins)]
    for step in range(1, sectors):
        mate(step).wait()
        total[...] += mates[step]

    @pl.when(slab > 0)
    def _():
        for step in range(sectors):
            beside(step, 0).wait_send()
            beside(step, 1).wait_recv()
            total[0:GHOSTS] += below[step]

    @pl.when(slab < slabs - 1)
    def _():
        for step in range(sectors):
            beside(step, 1).wait_send()
            beside(step, 0).wait_recv()
            total[pl.ds(bins - GHOSTS, GHOSTS)] += above[step]


def finish_kernel(force, base, mass, velocity_out, force_out, velocity, turned, done):
    for c in range(3):
        turned[c] = force[:, c, :]
    copy_force = pltpu.make_async_copy(turned, force_out, done.at[0])
    copy_force.start()
    for c in range(3):
        velocity[c] = base[c] + 0.5 * TIMESTEP * acceleration(turned[c], mass[...], c)
    copy_velocity = pltpu.make_async_copy(velocity, velocity_out, done.at[1])
    copy_velocity.start()
    copy_force.wait()
    copy_velocity.wait()


def solution(mesh):
    slabs, sectors = mesh.shape["slab"], mesh.shape["blk"]
    vmem = pl.BlockSpec(memory_space=pltpu.VMEM)
    smem = pl.BlockSpec(memory_space=pltpu.SMEM)
    hbm = pl.BlockSpec(memory_space=pltpu.HBM)

    def local(positions, radius, velocity, old_force, neighbours, tile_count):
        bins, _, spheres = positions.shape
        first_axis = lambda array: jnp.transpose(array, (1, 0, 2))
        slots = neighbours.shape[1]
        candidates = bins + 2 * GHOSTS
        ext, neigh_all, count_all, base, mass = pl.pallas_call(
            functools.partial(spread_kernel, slabs, sectors),
            out_shape=(
                jax.ShapeDtypeStruct((sectors, candidates, 4, spheres), jnp.float32),
                jax.ShapeDtypeStruct((sectors, slots, bins), jnp.int32),
                jax.ShapeDtypeStruct((sectors, 1, bins), jnp.int32),
                jax.ShapeDtypeStruct((3, bins, spheres), jnp.float32),
                jax.ShapeDtypeStruct((bins, spheres), jnp.float32),
            ),
            in_specs=[hbm] * 6,
            out_specs=(vmem,) * 5,
            scratch_shapes=[
                pltpu.VMEM((3, bins, spheres), jnp.float32),
                pltpu.VMEM((bins, spheres), jnp.float32),
                pltpu.VMEM((3, bins, spheres), jnp.float32),
                pltpu.VMEM((3, bins, spheres), jnp.float32),
                pltpu.SemaphoreType.DMA((5, sectors)),
                pltpu.SemaphoreType.DMA((5, sectors)),
                pltpu.SemaphoreType.DMA((6,)),
            ],
            compiler_params=pltpu.CompilerParams(
                collective_id=0, has_side_effects=True, vmem_limit_bytes=60 * 2**20
            ),
        )(
            first_axis(positions), radius, first_axis(velocity), first_axis(old_force),
            neighbours.T, tile_count.reshape(1, bins),
        )
        moved, react = pl.pallas_call(
            functools.partial(tiles_kernel, sectors),
            out_shape=(
                jax.ShapeDtypeStruct((3, bins, spheres), jnp.float32),
                jax.ShapeDtypeStruct((sectors, candidates + 1, 3, spheres), jnp.float32),
            ),
            in_specs=[smem, smem, vmem],
            out_specs=(hbm, vmem),
            scratch_shapes=[
                pltpu.VMEM((CHUNK, 5, spheres, spheres), jnp.float32),
                pltpu.VMEM((CHUNK, 3, spheres, spheres), jnp.float32),
                pltpu.VMEM((3, bins, spheres), jnp.float32),
                pltpu.SemaphoreType.DMA,
            ],
            compiler_params=pltpu.CompilerParams(vmem_limit_bytes=8 * 2**20),
        )(neigh_all, count_all, ext)
        force = pl.pallas_call(
            functools.partial(gather_kernel, slabs, sectors, bins),
            out_shape=jax.ShapeDtypeStruct((bins, 3, spheres), jnp.float32),
            in_specs=[vmem],
            out_specs=vmem,
            scratch_shapes=[
                pltpu.VMEM((sectors, bins, 3, spheres), jnp.float32),
                pltpu.VMEM((sectors, GHOSTS, 3, spheres), jnp.float32),
                pltpu.VMEM((sectors, GHOSTS, 3, spheres), jnp.float32),
                pltpu.SemaphoreType.DMA((3, sectors)),
                pltpu.SemaphoreType.DMA((3, sectors)),
            ],
            compiler_params=pltpu.CompilerParams(
                collective_id=1, has_side_effects=True, vmem_limit_bytes=8 * 2**20
            ),
        )(react)
        velocity_new, force_new = pl.pallas_call(
            finish_kernel,
            out_shape=(jax.ShapeDtypeStruct((3, bins, spheres), jnp.float32),) * 2,
            in_specs=[vmem] * 3,
            out_specs=(hbm, hbm),
            scratch_shapes=[
                pltpu.VMEM((3, bins, spheres), jnp.float32),
                pltpu.VMEM((3, bins, spheres), jnp.float32),
                pltpu.SemaphoreType.DMA((2,)),
            ],
            compiler_params=pltpu.CompilerParams(vmem_limit_bytes=8 * 2**20),
        )(force, base, mass)
        return (first_axis(moved), first_axis(velocity_new), first_axis(force_new))

    spec = P(("slab", "blk"))
    return jax.shard_map(
        local, mesh=mesh, in_specs=(spec,) * 6, out_specs=(spec,) * 3, check_vma=False
    )
```

```python
import functools

import jax
import jax.numpy as jnp
from jax import lax
from jax.experimental import pallas as pl
from jax.experimental.pallas import tpu as pltpu
from jax.sharding import PartitionSpec as P

GHOSTS = 8
STIFFNESS = 10.0
SOFTENING = 0.0025
TIMESTEP = 0.2
TINY = 1e-30
BIN_COST = 2
CHUNK = 4
MESH = pl.DeviceIdType.MESH


def acceleration(force, mass, component):
    accel = force / mass
    return accel - 0.5 if component == 1 else accel


def greet(slabs, sectors):
    slab, sector = lax.axis_index("slab"), lax.axis_index("blk")
    barrier = pltpu.get_barrier_semaphore()
    for step in range(1, sectors):
        other = lax.rem(sector + step, sectors)
        pl.semaphore_signal(barrier, inc=1, device_id=(slab, other), device_id_type=MESH)

    @pl.when(slab > 0)
    def _():
        for step in range(sectors):
            other = lax.rem(sector + step, sectors)
            pl.semaphore_signal(barrier, inc=1, device_id=(slab - 1, other), device_id_type=MESH)

    @pl.when(slab < slabs - 1)
    def _():
        for step in range(sectors):
            other = lax.rem(sector + step, sectors)
            pl.semaphore_signal(barrier, inc=1, device_id=(slab + 1, other), device_id_type=MESH)

    beside = jnp.where(slab > 0, sectors, 0) + jnp.where(slab < slabs - 1, sectors, 0)
    pl.semaphore_wait(barrier, sectors - 1 + beside)


def spread_kernel(
    slabs, sectors, pos_in, rad_in, vel_in, old_in, neigh_in, count_in,
    ext, neigh_all, count_all, base, mass, pos, rad, vel, old, send, recv, local,
):
    slab, sector = lax.axis_index("slab"), lax.axis_index("blk")
    bins = pos.shape[1]
    fetches = [
        pltpu.make_async_copy(source, target, local.at[index])
        for index, (source, target) in enumerate((
            (pos_in, pos), (rad_in, rad), (vel_in, vel), (old_in, old),
            (neigh_in, neigh_all.at[sector]), (count_in, count_all.at[sector]),
        ))
    ]
    for fetch in fetches:
        fetch.start()
    greet(slabs, sectors)
    for fetch in fetches:
        fetch.wait()
    radius = rad[...]
    mass[...] = 125.0 * radius * radius * radius
    accel_old = [acceleration(old[c], mass[...], c) for c in range(3)]
    for c in range(3):
        moved = pos[c] + TIMESTEP * vel[c] + 0.5 * TIMESTEP * TIMESTEP * accel_old[c]
        ext[sector, pl.ds(GHOSTS, bins), c : c + 1, :] = moved[:, None, :]
    ext[sector, pl.ds(GHOSTS, bins), 3:4, :] = radius[:, None, :]

    def mate(step, what):
        other = lax.rem(sector + step, sectors)
        ref = (ext.at[sector, pl.ds(GHOSTS, bins)], neigh_all.at[sector], count_all.at[sector])[what]
        return pltpu.make_async_remote_copy(
            src_ref=ref, dst_ref=ref, send_sem=send.at[what, step], recv_sem=recv.at[what, step],
            device_id=(slab, other), device_id_type=MESH,
        )

    def beside(step, up):
        other = lax.rem(sector + step, sectors)
        own_first = bins if up else GHOSTS
        there = 0 if up else GHOSTS + bins
        return pltpu.make_async_remote_copy(
            src_ref=ext.at[sector, pl.ds(own_first, GHOSTS)],
            dst_ref=ext.at[sector, pl.ds(there, GHOSTS)],
            send_sem=send.at[3 + up, step], recv_sem=recv.at[3 + up, step],
            device_id=(slab + (1 if up else -1), other), device_id_type=MESH,
        )

    for step in range(1, sectors):
        for what in range(3):
            mate(step, what).start()

    @pl.when(slab > 0)
    def _():
        for step in range(sectors):
            beside(step, 0).start()

    @pl.when(slab < slabs - 1)
    def _():
        for step in range(sectors):
            beside(step, 1).start()

    for c in range(3):
        base[c] = vel[c] + 0.5 * TIMESTEP * accel_old[c]
    for step in range(1, sectors):
        for what in range(3):
            mate(step, what).wait()

    @pl.when(slab > 0)
    def _():
        for step in range(sectors):
            beside(step, 0).wait_send()
            beside(step, 1).wait_recv()

    @pl.when(slab < slabs - 1)
    def _():
        for step in range(sectors):
            beside(step, 1).wait_send()
            beside(step, 0).wait_recv()


def tiles_kernel(sectors, neigh, count, ext, moved_out, react, acol, acc_one, acc_two, items, moved, done):
    sector = lax.axis_index("blk")
    bins = neigh.shape[2]
    spheres = ext.shape[3]
    strips = spheres // 8
    spare = bins + 2 * GHOSTS
    for c in range(3):
        moved[c] = ext[sector, pl.ds(GHOSTS, bins), c, :]
    store = pltpu.make_async_copy(moved, moved_out, done)
    store.start()
    react[...] = jnp.zeros_like(react)
    diagonal = lax.broadcasted_iota(jnp.int32, (spheres, spheres), 0) == lax.broadcasted_iota(
        jnp.int32, (spheres, spheres), 1
    )

    def fill_columns(slot, mine):
        wide = jnp.concatenate([mine, 0.01 / mine], axis=0).T
        for c, column in enumerate((0, 1, 2, 3, 7)):
            acol[slot, c] = jnp.broadcast_to(wide[:, column : column + 1], (spheres, spheres))
        for acc in (acc_one, acc_two):
            acc[slot] = jnp.zeros((3, spheres, spheres), jnp.float32)

    def row_sums(slot):
        return jnp.concatenate(
            [
                jnp.sum(
                    jnp.where(diagonal, jnp.sum(acc_one[slot, c] + acc_two[slot, c], axis=1, keepdims=True), 0.0),
                    axis=0, keepdims=True,
                )
                for c in range(3)
            ],
            axis=0,
        )

    def group_units(group):
        return lax.fori_loop(
            0, bins, lambda own, t: t + count[group, 0, own] + 1 + BIN_COST, 0, unroll=bins
        )

    sizes = [group_units(group) for group in range(sectors)]
    total = sum(sizes)
    first = total * sector // sectors
    last = total * (sector + 1) // sectors

    def run(group, first_item, how_many):
        places = [[items[row, first_item + step] for row in range(3)] for step in range(how_many)]
        rows_of = []
        for _, other, _ in places:
            values = ext[group, other]
            row = [jnp.broadcast_to(values[c : c + 1, :], (8, spheres)) for c in range(4)]
            rows_of.append(row + [0.01 / row[3]])
        totals = [[None] * 3 for _ in places]
        for strip in range(strips):
            rows = pl.ds(8 * strip, 8)
            for (slot, _, _), row, total_b, acc in zip(places, rows_of, totals, (acc_one, acc_two)):
                column = [acol[slot, c, rows, :] for c in range(5)]
                d = [column[c] - row[c] for c in range(3)]
                square = d[0] * d[0] + d[1] * d[1] + (d[2] * d[2] + SOFTENING)
                inverse = lax.rsqrt(square)
                overlap = jnp.maximum(column[3] + row[3] - square * inverse, TINY)
                stiff = lax.rsqrt(overlap * (column[4] + row[4]))
                pull = overlap * overlap * (inverse * stiff)
                for c in range(3):
                    w = pull * d[c]
                    total_b[c] = w if strip == 0 else total_b[c] + w
                    acc[slot, c, rows, :] += w
        sums = [
            jnp.concatenate([jnp.sum(t, axis=0, keepdims=True) for t in total_b], axis=0)
            for total_b in totals
        ]
        for (_, _, place), force in zip(places, sums):
            react[group, place] -= force

    def note_bin(group, chunk, slot, carry):
        start, size = carry
        own = chunk * CHUNK + slot
        tiles = count[group, 0, own] + 1
        low = jnp.maximum(first - start - BIN_COST, 0)
        high = jnp.maximum(jnp.minimum(last - start - BIN_COST, tiles), low)

        @pl.when((low == 0) & (high > 0))
        def _():
            items[0, size] = slot
            items[1, size] = GHOSTS + own
            items[2, size] = spare

        def note(k, _):
            other = neigh[group, k - 1, own]
            items[0, size + k - low] = slot
            items[1, size + k - low] = other
            items[2, size + k - low] = other
            return 0

        lax.fori_loop(jnp.maximum(low, 1), high, note, 0)
        return start + tiles + BIN_COST, size + high - low

    def one_chunk(group, chunk, start):
        stop = start
        for slot in range(CHUNK):
            stop += count[group, 0, chunk * CHUNK + slot] + 1 + BIN_COST

        @pl.when((stop > first) & (start < last))
        def _():
            here = GHOSTS + chunk * CHUNK
            for slot in range(CHUNK):
                fill_columns(slot, ext[group, here + slot])
            _, size = lax.fori_loop(
                0, CHUNK, functools.partial(note_bin, group, chunk), (start, 0)
            )

            def two(k, _):
                run(group, 2 * k, 2)
                return 0

            lax.fori_loop(0, size // 2, two, 0)

            @pl.when(size % 2 == 1)
            def _():
                run(group, size - 1, 1)

            sums = [row_sums(slot) for slot in range(CHUNK)]
            for slot in range(CHUNK):
                react[group, here + slot] += sums[slot]

        return stop

    def one_group(group, start):
        stop = start
        for other in range(sectors):
            stop += jnp.where(group == other, sizes[other], 0)
        touched = (stop > first) & (start < last)
        lax.fori_loop(
            0, jnp.where(touched, bins // CHUNK, 0), functools.partial(one_chunk, group), start
        )
        return stop

    lax.fori_loop(0, sectors, one_group, 0)
    store.wait()


def gather_kernel(slabs, sectors, bins, react, total, mates, below, above, send, recv):
    slab, sector = lax.axis_index("slab"), lax.axis_index("blk")
    greet(slabs, sectors)

    def mate(step):
        other = lax.rem(sector + step, sectors)
        return pltpu.make_async_remote_copy(
            src_ref=react.at[other, pl.ds(GHOSTS, bins)], dst_ref=mates.at[step],
            send_sem=send.at[0, step], recv_sem=recv.at[0, step],
            device_id=(slab, other), device_id_type=MESH,
        )

    def beside(step, up):
        other = lax.rem(sector + step, sectors)
        return pltpu.make_async_remote_copy(
            src_ref=react.at[other, pl.ds(GHOSTS + bins if up else 0, GHOSTS)],
            dst_ref=(below if up else above).at[step],
            send_sem=send.at[1 + up, step], recv_sem=recv.at[1 + up, step],
            device_id=(slab + (1 if up else -1), other), device_id_type=MESH,
        )

    for step in range(1, sectors):
        mate(step).start()

    @pl.when(slab > 0)
    def _():
        for step in range(sectors):
            beside(step, 0).start()

    @pl.when(slab < slabs - 1)
    def _():
        for step in range(sectors):
            beside(step, 1).start()

    total[...] = react[sector, pl.ds(GHOSTS, bins)]
    for step in range(1, sectors):
        mate(step).wait()
        total[...] += mates[step]

    @pl.when(slab > 0)
    def _():
        for step in range(sectors):
            beside(step, 0).wait_send()
            beside(step, 1).wait_recv()
            total[0:GHOSTS] += below[step]

    @pl.when(slab < slabs - 1)
    def _():
        for step in range(sectors):
            beside(step, 1).wait_send()
            beside(step, 0).wait_recv()
            total[pl.ds(bins - GHOSTS, GHOSTS)] += above[step]


def finish_kernel(force, base, mass, velocity_out, force_out, velocity, turned, done):
    for c in range(3):
        turned[c] = force[:, c, :]
    copy_force = pltpu.make_async_copy(turned, force_out, done.at[0])
    copy_force.start()
    for c in range(3):
        velocity[c] = base[c] + 0.5 * TIMESTEP * acceleration(turned[c], mass[...], c)
    copy_velocity = pltpu.make_async_copy(velocity, velocity_out, done.at[1])
    copy_velocity.start()
    copy_force.wait()
    copy_velocity.wait()


def solution(mesh):
    slabs, sectors = mesh.shape["slab"], mesh.shape["blk"]
    vmem = pl.BlockSpec(memory_space=pltpu.VMEM)
    smem = pl.BlockSpec(memory_space=pltpu.SMEM)
    hbm = pl.BlockSpec(memory_space=pltpu.HBM)

    def local(positions, radius, velocity, old_force, neighbours, tile_count):
        bins, _, spheres = positions.shape
        first_axis = lambda array: jnp.transpose(array, (1, 0, 2))
        slots = neighbours.shape[1]
        candidates = bins + 2 * GHOSTS
        ext, neigh_all, count_all, base, mass = pl.pallas_call(
            functools.partial(spread_kernel, slabs, sectors),
            out_shape=(
                jax.ShapeDtypeStruct((sectors, candidates, 4, spheres), jnp.float32),
                jax.ShapeDtypeStruct((sectors, slots, bins), jnp.int32),
                jax.ShapeDtypeStruct((sectors, 1, bins), jnp.int32),
                jax.ShapeDtypeStruct((3, bins, spheres), jnp.float32),
                jax.ShapeDtypeStruct((bins, spheres), jnp.float32),
            ),
            in_specs=[hbm] * 6,
            out_specs=(vmem,) * 5,
            scratch_shapes=[
                pltpu.VMEM((3, bins, spheres), jnp.float32),
                pltpu.VMEM((bins, spheres), jnp.float32),
                pltpu.VMEM((3, bins, spheres), jnp.float32),
                pltpu.VMEM((3, bins, spheres), jnp.float32),
                pltpu.SemaphoreType.DMA((5, sectors)),
                pltpu.SemaphoreType.DMA((5, sectors)),
                pltpu.SemaphoreType.DMA((6,)),
            ],
            compiler_params=pltpu.CompilerParams(
                collective_id=0, has_side_effects=True, vmem_limit_bytes=60 * 2**20
            ),
        )(
            first_axis(positions), radius, first_axis(velocity), first_axis(old_force),
            neighbours.T, tile_count.reshape(1, bins),
        )
        moved, react = pl.pallas_call(
            functools.partial(tiles_kernel, sectors),
            out_shape=(
                jax.ShapeDtypeStruct((3, bins, spheres), jnp.float32),
                jax.ShapeDtypeStruct((sectors, candidates + 1, 3, spheres), jnp.float32),
            ),
            in_specs=[smem, smem, vmem],
            out_specs=(hbm, vmem),
            scratch_shapes=[
                pltpu.VMEM((CHUNK, 5, spheres, spheres), jnp.float32),
                pltpu.VMEM((CHUNK, 3, spheres, spheres), jnp.float32),
                pltpu.VMEM((CHUNK, 3, spheres, spheres), jnp.float32),
                pltpu.SMEM((3, CHUNK * (slots + 1)), jnp.int32),
                pltpu.VMEM((3, bins, spheres), jnp.float32),
                pltpu.SemaphoreType.DMA,
            ],
            compiler_params=pltpu.CompilerParams(vmem_limit_bytes=8 * 2**20),
        )(neigh_all, count_all, ext)
        force = pl.pallas_call(
            functools.partial(gather_kernel, slabs, sectors, bins),
            out_shape=jax.ShapeDtypeStruct((bins, 3, spheres), jnp.float32),
            in_specs=[vmem],
            out_specs=vmem,
            scratch_shapes=[
                pltpu.VMEM((sectors, bins, 3, spheres), jnp.float32),
                pltpu.VMEM((sectors, GHOSTS, 3, spheres), jnp.float32),
                pltpu.VMEM((sectors, GHOSTS, 3, spheres), jnp.float32),
                pltpu.SemaphoreType.DMA((3, sectors)),
                pltpu.SemaphoreType.DMA((3, sectors)),
            ],
            compiler_params=pltpu.CompilerParams(
                collective_id=1, has_side_effects=True, vmem_limit_bytes=8 * 2**20
            ),
        )(react)
        velocity_new, force_new = pl.pallas_call(
            finish_kernel,
            out_shape=(jax.ShapeDtypeStruct((3, bins, spheres), jnp.float32),) * 2,
            in_specs=[vmem] * 3,
            out_specs=(hbm, hbm),
            scratch_shapes=[
                pltpu.VMEM((3, bins, spheres), jnp.float32),
                pltpu.VMEM((3, bins, spheres), jnp.float32),
                pltpu.SemaphoreType.DMA((2,)),
            ],
            compiler_params=pltpu.CompilerParams(vmem_limit_bytes=8 * 2**20),
        )(force, base, mass)
        return (first_axis(moved), first_axis(velocity_new), first_axis(force_new))

    spec = P(("slab", "blk"))
    return jax.shard_map(
        local, mesh=mesh, in_specs=(spec,) * 6, out_specs=(spec,) * 3, check_vma=False
    )
```
